256 devices in a mesh: lon: 64 (over z, x, y_hi), lat: 4 (over y_lo, core).
Axes of the slice: x: 4, y: 4 (y_hi: 2, y_lo: 2; y = y_hi * 2 + y_lo), z: 8, core: 2. Of those that a mesh axis runs over, the one named last changes fastest.
Arguments:
- stored_blocks: bfloat16 [3, 4096, 2048], P(None, 'lon', 'lat'), may hold values from -2.5 to 2.5
- row_scale: float32 [3, 2048], P(None, 'lat'), may hold values from 0.05 to 0.5
- levels: int32 [4096, 2048], P('lon', 'lat'), may hold values from 1 to 75
- land_mask: int32 [4096, 2048], P('lon', 'lat'), may hold values 0 or 1
- cotangent: float32 [3, 4096, 2048], P(None, 'lon', 'lat'), may hold values from -6 to 6
Outputs:
- checkpoint_grad: float32 [3, 4096, 2048], P(None, 'lon', 'lat')
- scale_grad: float32 [3, 2048], P(None, 'lat')
The draws below stay inside these ranges and needn't reach their ends.
All inputs are finite; a program needn't handle non-finite values. No bound on the sum of `land_mask` on one device may be relied on, other than what follows from the above.
Results may differ from the reference program's by a relative error of at most 0.0003.
Values sent between devices are 32-bit elements; how exact they have to be, the bound alone decides.
No kernel may reach another device: no remote copies, remote signals or barrier semaphores. Data moves between devices by JAX's collectives and lax.ppermute only.
A program may use at most 64 MiB of HBM per device.

```python
import math
import jax
import jax.numpy as jnp
from jax import lax

STEPS = 4
NX = 4096
NY = 2048


def with_ends(values, stream_key, smallest, largest):
    longest = values.shape.index(max(values.shape))
    spots = []
    for shift in (0, 1):
        where = [jax.random.randint(jax.random.fold_in(stream_key, axis), (), 0, length) for axis, length in enumerate(values.shape)]
        where[longest] = (where[longest] + shift) % values.shape[longest]
        spots.append(tuple(where))
    return values.at[spots[0]].set(smallest).at[spots[1]].set(largest)


def steps_of(stream_key, dims, pieces, low, largest):
    gain = 1.0
    for position, parts in pieces:
        draws = jax.random.uniform(jax.random.fold_in(jax.random.fold_in(stream_key, 6), position), (parts,), jnp.float32, low / len(pieces), largest / len(pieces))
        gain = gain * jnp.repeat(jnp.exp(draws), dims[position] // parts).reshape((-1,) + (1,) * (len(dims) - 1 - position))
    return gain


def noise(own_key, extent, deviation, most, pieces=(), held_as=jnp.bfloat16):
    drawn = jax.random.normal(own_key, extent, jnp.float32) * deviation
    if len(pieces) > 0:
        drawn = steps_of(own_key, extent, pieces, -0.22, 0.18) * drawn
    return jnp.clip(drawn, min=-most, max=most).astype(held_as)


def setup_inputs(seed: int = 0) -> dict:
    key_list = jax.random.split(jax.random.key(seed), 6)
    return {
        "stored_blocks": noise(key_list[0], (3, NX, NY), 0.5, 2.5, ((1, 64), (2, 4))),
        "row_scale": jnp.clip(jnp.exp(math.log(0.5) - 2.3025851 * jax.random.uniform(key_list[1], (3, NY), jnp.float32) ** steps_of(key_list[1], (3, NY), ((1, 4),), -0.2, 0.2)), 0.05, 0.5),
        "levels": with_ends(jax.random.randint(key_list[2], (NX, NY), 1, 76), jax.random.fold_in(key_list[2], 1), 1, 75).astype(jnp.int32),
        "land_mask": with_ends((jax.random.randint(key_list[3], (NX, NY), 0, 10) < 9).astype(jnp.int32), jax.random.fold_in(key_list[3], 1), 0, 1),
        "cotangent": noise(key_list[4], (3, NX, NY), 0.5, 6.0, ((1, 64), (2, 4)), jnp.float32),
    }


time_step = 0.5
gravity = 1.0
level_depth = 0.08
damping = 0.02
coriolis = 0.1

def advance(current, ocean_mask, floor_depth, spin_rows):
    height = current[0]
    east_speed = current[1]
    north_speed = current[2]
    column_depth = floor_depth + height
    flux_east = ocean_mask * column_depth * east_speed
    flux_north = ocean_mask * column_depth * north_speed
    diverge = 0.5 * (flux_east[2:, 1:-1] - flux_east[:-2, 1:-1] + flux_north[1:-1, 2:] - flux_north[1:-1, :-2])
    surface = height[1:-1, 1:-1] - time_step * ocean_mask[1:-1, 1:-1] * diverge
    slope_east = 0.5 * (surface[2:, 1:-1] - surface[:-2, 1:-1])
    slope_north = 0.5 * (surface[1:-1, 2:] - surface[1:-1, :-2])
    ocean_inner = ocean_mask[2:-2, 2:-2]
    spin_inner = spin_rows[2:-2]
    old_east = east_speed[2:-2, 2:-2]
    old_north = north_speed[2:-2, 2:-2]
    new_east = ocean_inner * ((1.0 - damping) * old_east - time_step * gravity * slope_east + time_step * spin_inner * old_north)
    new_north = ocean_inner * ((1.0 - damping) * old_north - time_step * gravity * slope_north - time_step * spin_inner * old_east)
    return jnp.stack([surface[1:-1, 1:-1], new_east, new_north])

def spin_table(first_row, row_count, total_rows):
    row_place = first_row + jnp.arange(row_count, dtype=jnp.float32)
    return coriolis * jnp.cos(math.pi * (row_place + 0.5 - total_rows) / (2.0 * total_rows))

def extend_global(fields, flip_signs, margin):
    wrapped = jnp.concatenate([fields[:, -margin:], fields, fields[:, :margin]], axis=1)
    south_rows = jnp.zeros(wrapped.shape[:2] + (margin,), jnp.float32)
    north_rows = jnp.flip(wrapped[:, :, -margin:], axis=(1, 2)) * flip_signs[:, None, None]
    return jnp.concatenate([south_rows, wrapped, north_rows], axis=2)

def reference(stored_blocks, row_scale, levels, land_mask, cotangent):
    initial = stored_blocks.astype(jnp.float32) * row_scale[:, None, :]
    statics = jnp.stack([land_mask.astype(jnp.float32), level_depth * levels.astype(jnp.float32)])
    statics_ext = extend_global(statics, jnp.ones((2,), jnp.float32), 2)
    spin_rows = spin_table(-2.0, NY + 4, NY)
    state_signs = jnp.array([1.0, -1.0, -1.0], jnp.float32)

    def subcycle(current):
        return advance(extend_global(current, state_signs, 2), statics_ext[0], statics_ext[1], spin_rows)
    guarded = jax.checkpoint(subcycle)

    def forward(current):
        for repeat in range(STEPS):
            current = guarded(current)
        return current
    _, pullback = jax.vjp(forward, initial)
    adjoint = pullback(cotangent)[0]
    checkpoint_grad = adjoint * row_scale[:, None, :]
    scale_grad = lax.optimization_barrier(jnp.sum(adjoint * stored_blocks.astype(jnp.float32), axis=1))
    return (checkpoint_grad, scale_grad)
```

```python
import math

import jax
import jax.numpy as jnp
from jax import lax
from jax.experimental import pallas as pl
from jax.experimental.pallas import tpu as pltpu
from jax.sharding import PartitionSpec as P

STEPS = 4
GRAVITY = 1.0
TIME_STEP = 0.5
LEVEL_DEPTH = 0.08
KEEP = 1.0 - 0.02
CORIOLIS = 0.1
HALF = 0.5 * TIME_STEP

COLS = 64
ROWS = 512
LANES = 128
TILES = ROWS // LANES
WIDE = 12
THIN = 8
BASE = 24
HEIGHT = 112
PACK = 88

WIDTHS = (WIDE,) * 5 + (THIN,) * 3
PLACES = tuple(sum(WIDTHS[:f]) for f in range(8))
SIGNS = (1.0, 1.0, 1.0, -1.0, -1.0, 1.0, -1.0, -1.0)


def lanes_of(shape):
    return lax.broadcasted_iota(jnp.int32, shape, len(shape) - 1)


def own_fields(stored, scale, levels, mask, cot):
    ocean = mask.astype(jnp.float32)
    floor = ocean * (LEVEL_DEPTH * levels.astype(jnp.float32))
    state = [stored[k].astype(jnp.float32) * scale[k : k + 1] for k in range(3)]
    return [ocean, floor] + state + [cot[0], ocean * cot[1], ocean * cot[2]]


def lon_pack_kernel(
    st_lo, st_hi, scale, lev_lo, lev_hi, mask_lo, mask_hi, cot_lo, cot_hi, a_ref, b_ref
):
    odd = lax.rem(lax.axis_index("lon"), 2) == 1
    low = own_fields(st_lo[...], scale[...], lev_lo[...], mask_lo[...], cot_lo[...])
    high = own_fields(st_hi[...], scale[...], lev_hi[...], mask_hi[...], cot_hi[...])
    for f in range(8):
        width, place = WIDTHS[f], PLACES[f]
        lower, upper = low[f][:width], high[f][16 - width :]
        a_ref[place : place + width] = jnp.where(odd, lower, upper)
        b_ref[place : place + width] = jnp.where(odd, upper, lower)
    a_ref[84:88] = jnp.zeros((4, ROWS), jnp.float32)
    b_ref[84:88] = jnp.zeros((4, ROWS), jnp.float32)


def lon_pack(stored, scale, levels, mask, cot):
    last = COLS // 16 - 1
    three = [pl.BlockSpec((3, 16, ROWS), lambda _, b=b: (0, b, 0)) for b in (0, last)]
    one = [pl.BlockSpec((16, ROWS), lambda _, b=b: (b, 0)) for b in (0, last)]
    out = jax.ShapeDtypeStruct((PACK, ROWS), jnp.float32)
    return pl.pallas_call(
        lon_pack_kernel,
        grid=(1,),
        in_specs=[*three, pl.BlockSpec((3, ROWS), lambda _: (0, 0)), *one, *one, *three],
        out_specs=[pl.BlockSpec((PACK, ROWS), lambda _: (0, 0))] * 2,
        out_shape=[out, out],
        name="lon_pack",
    )(stored, stored, scale, levels, levels, mask, mask, cot, cot)


def lat_pack_kernel(
    st_s, st_n, sc_s, sc_n, lev_s, lev_n, mask_s, mask_n, cot_s, cot_n, a_s, a_n, b_s, b_n,
    out_a, out_b, south, north,
):
    odd = lax.rem(lax.axis_index("lon"), 2) == 1
    lat = lax.axis_index("lat")
    upper = lax.rem(lat, 2) == 1
    top = lat == lax.axis_size("lat") - 1

    def pack(fields, to_south):
        total = jnp.zeros((fields[0].shape[0], LANES), jnp.float32)
        lane = lanes_of(total.shape)
        for f in range(8):
            width, place = WIDTHS[f], PLACES[f]
            shift = place if to_south else (place + width) % LANES
            moved = fields[f] if shift == 0 else pltpu.roll(fields[f], shift, 1)
            total = jnp.where((lane >= place) & (lane < place + width), moved, total)
        return total

    for dst, st, sc, lev, mask, cot, a, b, to_south in (
        (south, st_s, sc_s, lev_s, mask_s, cot_s, a_s, b_s, True),
        (north, st_n, sc_n, lev_n, mask_n, cot_n, a_n, b_n, False),
    ):
        dst[WIDE : WIDE + COLS] = pack(
            own_fields(st[...], sc[...], lev[...], mask[...], cot[...]), to_south
        )
        for side in range(2):
            fields = []
            for f in range(8):
                rows = pl.ds(PLACES[f], WIDTHS[f])
                piece = jnp.where(odd == (side == 0), a[rows], b[rows])
                if WIDTHS[f] < WIDE:
                    gap = jnp.zeros((WIDE - WIDTHS[f], LANES), jnp.float32)
                    piece = jnp.concatenate([gap, piece] if side == 0 else [piece, gap], axis=0)
                fields.append(piece)
            start = 0 if side == 0 else WIDE + COLS
            dst[start : start + WIDE] = pack(fields, to_south)
    out_a[...] = jnp.where(upper, south[...], north[...])
    out_b[...] = jnp.where(upper, north[...], south[...])

    @pl.when(top)
    def _():
        i = lax.broadcasted_iota(jnp.int32, (PACK, PACK), 0)
        j = lax.broadcasted_iota(jnp.int32, (PACK, PACK), 1)
        flip_cols = jnp.where(i + j == PACK - 1, 1.0, 0.0)
        i = lax.broadcasted_iota(jnp.int32, (LANES, LANES), 0)
        j = lax.broadcasted_iota(jnp.int32, (LANES, LANES), 1)
        flip_rows = jnp.zeros((LANES, LANES), jnp.float32)
        for f in range(8):
            first, last = PLACES[f], PLACES[f] + WIDTHS[f] - 1
            here = (i >= first) & (i <= last) & (i + j == first + last)
            flip_rows = jnp.where(here, SIGNS[f], flip_rows)
        exact = dict(precision=lax.Precision.HIGHEST, preferred_element_type=jnp.float32)
        out_b[...] = jnp.dot(flip_cols, jnp.dot(north[...], flip_rows, **exact), **exact)


def lat_pack(stored, scale, levels, mask, cot, from_a, from_b):
    ends = (0, TILES - 1)
    three = [pl.BlockSpec((3, COLS, LANES), lambda _, b=b: (0, 0, b)) for b in ends]
    scales = [pl.BlockSpec((3, LANES), lambda _, b=b: (0, b)) for b in ends]
    one = [pl.BlockSpec((COLS, LANES), lambda _, b=b: (0, b)) for b in ends]
    margin = [pl.BlockSpec((PACK, LANES), lambda _, b=b: (0, b)) for b in ends]
    out = jax.ShapeDtypeStruct((PACK, LANES), jnp.float32)
    return pl.pallas_call(
        lat_pack_kernel,
        grid=(1,),
        in_specs=[*three, *scales, *one, *one, *three, *margin, *margin],
        out_specs=[pl.BlockSpec((PACK, LANES), lambda _: (0, 0))] * 2,
        out_shape=[out, out],
        scratch_shapes=[pltpu.VMEM((PACK, LANES), jnp.float32)] * 2,
        name="lat_pack",
    )(
        stored, stored, scale, scale, levels, levels, mask, mask, cot, cot,
        from_a, from_a, from_b, from_b,
    )


def main_kernel(
    stored, scale, levels, mask, cot, spin, lon_a, lon_b, lat_a, lat_b,
    grad, partial,
    m, m0, u0, u1, u2, u3, v0, v1, v2, v3, w0, w1, w2, w3, ea, eb, fe, q, la, lb, le,
):
    odd = lax.rem(lax.axis_index("lon"), 2) == 1
    upper = lax.rem(lax.axis_index("lat"), 2) == 1
    us, vs, ws = (u0, u1, u2, u3), (v0, v1, v2, v3), (w0, w1, w2, w3)
    fields = (m, m0, ea, u0, v0, le, la, lb)
    every = TILES + 1

    for f in range(8):
        for row in (slice(0, 16), slice(96, HEIGHT)):
            fields[f][:, row] = jnp.zeros((every, 16, LANES), jnp.float32)
        fields[f][TILES, 16:96] = jnp.zeros((80, LANES), jnp.float32)
    for t in range(TILES):
        at = slice(t * LANES, (t + 1) * LANES)
        own = own_fields(
            stored[:, :, at], scale[:, at], levels[:, at], mask[:, at], cot[:, :, at]
        )
        for f in range(8):
            fields[f][t, BASE : BASE + COLS] = own[f]
            width, rows = WIDTHS[f], slice(PLACES[f], PLACES[f] + WIDTHS[f])
            from_a, from_b = lon_a[rows, at], lon_b[rows, at]
            fields[f][t, BASE - width : BASE] = jnp.where(odd, from_a, from_b)
            fields[f][t, BASE + COLS : BASE + COLS + width] = jnp.where(odd, from_b, from_a)
    north = jnp.where(upper, lat_b[...], lat_a[...])
    south = jnp.where(upper, lat_a[...], lat_b[...])
    lane = lanes_of((PACK, LANES))
    for f in range(8):
        width, place = WIDTHS[f], PLACES[f]
        up = pltpu.roll(north, (LANES - place) % LANES, 1) if place else north
        down = pltpu.roll(south, LANES - width - place, 1)
        edge = jnp.where(lane < width, up, jnp.where(lane >= LANES - width, down, 0.0))
        fields[f][TILES, BASE - WIDE : BASE + COLS + WIDE] = edge

    first = lanes_of((every, 8, LANES)) == 0
    final = lanes_of((every, 8, LANES)) == LANES - 1

    def lat_diff(x):
        ahead = pltpu.roll(x, LANES - 1, 2)
        behind = pltpu.roll(x, 1, 2)
        ahead = jnp.where(final, jnp.concatenate([ahead[1:], ahead[:1]], axis=0), ahead)
        behind = jnp.where(first, jnp.concatenate([behind[-1:], behind[:-1]], axis=0), behind)
        return ahead - behind

    def lon_diff(ref, r):
        return ref[:, pl.ds(r + 1, 8)] - ref[:, pl.ds(r - 1, 8)]

    def sweep(start, stop, body):
        for r in range(start, stop, 8):
            body(r, pl.ds(r, 8))

    turn = spin[...]

    def start_step(r, here):
        w = m0[:, here] + m[:, here] * ea[:, here]
        w0[:, here] = w
        fe[:, here] = w * u0[:, here]

    sweep(8, 104, start_step)

    for k in range(STEPS - 1):
        e, s = (ea, eb) if k % 2 == 0 else (eb, ea)
        u, v, w, u_next, v_next, w_next = us[k], vs[k], ws[k], us[k + 1], vs[k + 1], ws[k + 1]
        lo, hi = ((8, 104), (8, 104), (16, 96))[k]
        lo_s, hi_s = ((8, 104), (8, 104), (16, 96))[k]
        if k == 1:
            lo, hi = 16, 96

        def height_pass(r, here):
            diverge = lon_diff(fe, r) + lat_diff(w[:, here] * v[:, here])
            s[:, here] = e[:, here] - (HALF * m[:, here]) * diverge

        sweep(lo_s, hi_s, height_pass)

        def speed_pass(r, here):
            ocean, height = m[:, here], s[:, here]
            old_u, old_v = u[:, here], v[:, here]
            new_u = ocean * (KEEP * old_u + turn * old_v - (GRAVITY * HALF) * lon_diff(s, r))
            new_v = ocean * (KEEP * old_v - turn * old_u - (GRAVITY * HALF) * lat_diff(height))
            u_next[:, here] = new_u
            v_next[:, here] = new_v
            new_w = m0[:, here] + ocean * height
            w_next[:, here] = new_w
            if k < STEPS - 2:
                fe[:, here] = new_w * new_u

        sweep(lo, hi, speed_pass)

    sums = [jnp.zeros((TILES, 8, LANES), jnp.float32) for _ in range(3)]
    for k in reversed(range(STEPS)):
        u, v, w, sb = us[k], vs[k], ws[k], fe

        def height_back(r, here):
            back = le[:, here] + (GRAVITY * HALF) * (lon_diff(la, r) + lat_diff(lb[:, here]))
            sb[:, here] = back
            q[:, here] = (HALF * m[:, here]) * back

        sweep(16, 96, height_back)

        def speed_back(r, here):
            g = lon_diff(q, r)
            h = lat_diff(q[:, here])
            a, b, depth = la[:, here], lb[:, here], w[:, here]
            new_a = KEEP * a - turn * b + depth * g
            new_b = KEEP * b + turn * a + depth * h
            new_e = sb[:, here] + m[:, here] * (u[:, here] * g + v[:, here] * h)
            if k > 0:
                la[:, here] = new_a
                lb[:, here] = new_b
                le[:, here] = new_e
                return
            own = slice(r - BASE, r - BASE + 8)
            for n, new in enumerate((new_e, new_a, new_b)):
                for t in range(TILES):
                    at = slice(t * LANES, (t + 1) * LANES)
                    grad[n, own, at] = new[t] * scale[n : n + 1, at]
            half = (r - BASE) // 16 * 16
            for n, new in enumerate((new_e, new_a, new_b)):
                parts = []
                for t in range(TILES):
                    at = slice(t * LANES, (t + 1) * LANES)
                    block = stored[n, half : half + 16, at].astype(jnp.float32)
                    parts.append(new[t] * block[r - BASE - half : r - BASE - half + 8])
                sums[n] = sums[n] + jnp.stack(parts)

        if k > 0:
            sweep(16, 96, speed_back)
        else:
            sweep(BASE, BASE + COLS, speed_back)
    for n in range(3):
        partial[4 * n : 4 * n + 4] = jnp.sum(sums[n], axis=1)


def main(stored, scale, levels, mask, cot, spin, lon_a, lon_b, lat_a, lat_b):
    big = pltpu.VMEM((TILES + 1, HEIGHT, LANES), jnp.float32)
    return pl.pallas_call(
        main_kernel,
        in_specs=[pl.BlockSpec(memory_space=pltpu.VMEM)] * 10,
        out_specs=[pl.BlockSpec(memory_space=pltpu.VMEM)] * 2,
        out_shape=[
            jax.ShapeDtypeStruct((3, COLS, ROWS), jnp.float32),
            jax.ShapeDtypeStruct((3 * TILES, LANES), jnp.float32),
        ],
        scratch_shapes=[big] * 21,
        compiler_params=pltpu.CompilerParams(vmem_limit_bytes=32 * 2**20),
        name="main",
    )(stored, scale, levels, mask, cot, spin, lon_a, lon_b, lat_a, lat_b)


def spin_table():
    total = ROWS * lax.axis_size("lat")
    lane = jnp.arange((TILES + 1) * LANES, dtype=jnp.int32)
    row = jnp.where(lane < ROWS + LANES // 2, lane, lane - (TILES + 1) * LANES)
    row = (row + lax.axis_index("lat") * ROWS).astype(jnp.float32)
    spin = CORIOLIS * jnp.cos(math.pi * (row + 0.5 - total) / (2.0 * total))
    spin = jnp.broadcast_to((TIME_STEP * spin).reshape(TILES + 1, 1, LANES), (TILES + 1, 8, LANES))
    return spin


def sum_over_lon(value):
    size = lax.axis_size("lon")
    step = 1
    while step < size:
        value = value + lax.ppermute(value, "lon", [(s, s ^ step) for s in range(size)])
        step *= 2
    return value


def shards(stored, scale, levels, mask, cot):
    lons, lats = lax.axis_size("lon"), lax.axis_size("lat")
    to_a, to_b = lon_pack(stored, scale, levels, mask, cot)
    lon_a = lax.ppermute(to_a, "lon", [(s, s ^ 1) for s in range(lons)])
    lon_b = lax.ppermute(
        to_b, "lon", [(s, (s + 1) % lons if s % 2 else (s - 1) % lons) for s in range(lons)]
    )
    to_a, to_b = lat_pack(stored, scale, levels, mask, cot, lon_a, lon_b)
    lat_a = lax.ppermute(to_a, "lat", [(s, s ^ 1) for s in range(lats)])
    pairs = []
    for l in range(lons):
        for t in range(1, lats - 1, 2):
            pairs += [(l * lats + t, l * lats + t + 1), (l * lats + t + 1, l * lats + t)]
        pairs.append((l * lats + lats - 1, (lons - 1 - l) * lats + lats - 1))
    lat_b = lax.ppermute(to_b, ("lon", "lat"), pairs)
    grad, partial = main(
        stored, scale, levels, mask, cot, spin_table(), lon_a, lon_b, lat_a, lat_b
    )
    return grad, sum_over_lon(partial).reshape(3, ROWS)


def solution(mesh):
    return jax.shard_map(
        shards,
        mesh=mesh,
        in_specs=(
            P(None, "lon", "lat"),
            P(None, "lat"),
            P("lon", "lat"),
            P("lon", "lat"),
            P(None, "lon", "lat"),
        ),
        out_specs=(P(None, "lon", "lat"), P(None, "lat")),
        check_vma=False,
    )
```

```python
import math

import jax
import jax.numpy as jnp
from jax import lax
from jax.experimental import pallas as pl
from jax.experimental.pallas import tpu as pltpu
from jax.sharding import PartitionSpec as P

STEPS = 4
GRAVITY = 1.0
TIME_STEP = 0.5
LEVEL_DEPTH = 0.08
KEEP = 1.0 - 0.02
CORIOLIS = 0.1
HALF = 0.5 * TIME_STEP

COLS = 64
ROWS = 512
LANES = 128
TILES = ROWS // LANES
WIDE = 11
BASE = 24
HEIGHT = 112
SIDE = 76
BULK = SIDE * TILES

LON_WIDTHS = (11, 11, 11, 11, 10, 7, 8, 7)
LAT_WIDTHS = (11, 11, 11, 10, 11, 7, 7, 8)
LON_PLACES = tuple(sum(LON_WIDTHS[:f]) for f in range(8))
LAT_PLACES = tuple(sum(LAT_WIDTHS[:f]) for f in range(8))
SIGNS = (1.0, 1.0, 1.0, -1.0, -1.0, 1.0, -1.0, -1.0)
VMEM = pl.BlockSpec(memory_space=pltpu.VMEM)
SMALL = pltpu.CompilerParams(vmem_limit_bytes=4 * 2**20)


def lanes_of(shape):
    return lax.broadcasted_iota(jnp.int32, shape, len(shape) - 1)


def own_fields(stored, scale, levels, mask, cot):
    ocean = mask.astype(jnp.float32)
    floor = ocean * (LEVEL_DEPTH * levels.astype(jnp.float32))
    state = [stored[k].astype(jnp.float32) * scale[k : k + 1] for k in range(3)]
    return [ocean, floor] + state + [cot[0], ocean * cot[1], ocean * cot[2]]


def lat_pack_kernel(
    stored, scale, levels, mask, cot, out_a, out_b, st, sc, lev, ocean, adj, sems
):
    arrays = ((stored, st), (scale, sc), (levels, lev), (mask, ocean), (cot, adj))
    copies = []
    for tile in (0, TILES - 1):
        for n, (src, dst) in enumerate(arrays):
            side = min(tile, 1)
            at = pl.ds(tile * LANES, LANES)
            copies.append(
                pltpu.make_async_copy(
                    src.at[(slice(None),) * (len(src.shape) - 1) + (at,)],
                    dst.at[side],
                    sems.at[side, n],
                )
            )
    for copy in copies:
        copy.start()
    lat = lax.axis_index("lat")
    upper = lax.rem(lat, 2) == 1
    top = lat == lax.axis_size("lat") - 1
    for copy in copies:
        copy.wait()
    packs = []
    for side, to_south in ((0, True), (1, False)):
        fields = own_fields(st[side], sc[side], lev[side], ocean[side], adj[side])
        total = jnp.zeros((COLS, LANES), jnp.float32)
        lane = lanes_of(total.shape)
        for f in range(8):
            width, place = LAT_WIDTHS[f], LAT_PLACES[f]
            shift = place if to_south else (place + width) % LANES
            moved = fields[f] if shift == 0 else pltpu.roll(fields[f], shift, 1)
            total = jnp.where((lane >= place) & (lane < place + width), moved, total)
        packs.append(total)
    south, north = packs
    out_a[...] = jnp.where(upper, south, north)
    out_b[...] = jnp.where(upper, north, south)

    @pl.when(top)
    def _():
        i = lax.broadcasted_iota(jnp.int32, (COLS, COLS), 0)
        j = lax.broadcasted_iota(jnp.int32, (COLS, COLS), 1)
        flip_cols = jnp.where(i + j == COLS - 1, 1.0, 0.0)
        i = lax.broadcasted_iota(jnp.int32, (LANES, LANES), 0)
        j = lax.broadcasted_iota(jnp.int32, (LANES, LANES), 1)
        flip_rows = jnp.zeros((LANES, LANES), jnp.float32)
        for f in range(8):
            first, last = LAT_PLACES[f], LAT_PLACES[f] + LAT_WIDTHS[f] - 1
            here = (i >= first) & (i <= last) & (i + j == first + last)
            flip_rows = jnp.where(here, SIGNS[f], flip_rows)
        exact = dict(precision=lax.Precision.HIGHEST, preferred_element_type=jnp.float32)
        out_b[...] = jnp.dot(flip_cols, jnp.dot(out_b[...], flip_rows, **exact), **exact)


def lat_pack(*own):
    out = jax.ShapeDtypeStruct((COLS, LANES), jnp.float32)
    return pl.pallas_call(
        lat_pack_kernel,
        in_specs=[pl.BlockSpec(memory_space=pltpu.HBM)] * 5,
        out_specs=[VMEM] * 2,
        out_shape=[out, out],
        scratch_shapes=[
            pltpu.VMEM((2, 3, COLS, LANES), jnp.bfloat16),
            pltpu.VMEM((2, 3, LANES), jnp.float32),
            pltpu.VMEM((2, COLS, LANES), jnp.int32),
            pltpu.VMEM((2, COLS, LANES), jnp.int32),
            pltpu.VMEM((2, 3, COLS, LANES), jnp.float32),
            pltpu.SemaphoreType.DMA((2, 5)),
        ],
        compiler_params=pltpu.CompilerParams(vmem_limit_bytes=55100 * 2**10),
        name="lat_pack",
    )(*own)


def lon_pack_kernel(*refs):
    srcs, (a_ref, b_ref), dsts, sems = refs[:5], refs[6:8], refs[8:13], refs[13]
    copies = [pltpu.make_async_copy(srcs[n], dsts[n], sems.at[n]) for n in range(5)]
    for copy in copies:
        copy.start()
    odd = lax.rem(lax.axis_index("lon"), 2) == 1
    for copy in copies:
        copy.wait()
    stored, scale, levels, mask, cot = dsts
    for t in range(TILES):
        at = slice(t * LANES, (t + 1) * LANES)
        low, high = (
            own_fields(
                stored[:, cut, at], scale[:, at], levels[cut, at], mask[cut, at], cot[:, cut, at]
            )
            for cut in (slice(0, 16), slice(COLS - 16, COLS))
        )
        for f in range(8):
            width, place = LON_WIDTHS[f], t * SIDE + LON_PLACES[f]
            lower, upper = low[f][:width], high[f][16 - width :]
            a_ref[place : place + width] = jnp.where(odd, lower, upper)
            b_ref[place : place + width] = jnp.where(odd, upper, lower)


def lon_pack(own, after):
    out = jax.ShapeDtypeStruct((BULK, LANES), jnp.float32)
    outs = pl.pallas_call(
        lon_pack_kernel,
        in_specs=[pl.BlockSpec(memory_space=pltpu.HBM)] * 6,
        out_specs=[VMEM] * 7,
        out_shape=[out, out] + [jax.ShapeDtypeStruct(x.shape, x.dtype) for x in own],
        scratch_shapes=[pltpu.SemaphoreType.DMA((5,))],
        compiler_params=SMALL,
        name="lon_pack",
        cost_estimate=pl.CostEstimate(flops=10**6, bytes_accessed=10**6, transcendentals=0),
    )(*own, after)
    return outs[:2], outs[2:]


def corner_pack_kernel(lat_a, lat_b, a_in, b_in, a_ref, b_ref):
    odd = lax.rem(lax.axis_index("lon"), 2) == 1
    for n, margin in enumerate((lat_a, lat_b)):
        lower, upper = margin[:WIDE], margin[COLS - WIDE :]
        rows = slice(BULK + n * WIDE, BULK + (n + 1) * WIDE)
        a_ref[rows] = jnp.where(odd, lower, upper)
        b_ref[rows] = jnp.where(odd, upper, lower)
    for src, ref in ((a_in, a_ref), (b_in, b_ref)):
        ref[:BULK] = src[...]
        ref[BULK + 2 * WIDE :] = jnp.zeros((24 - 2 * WIDE, LANES), jnp.float32)


def corner_pack(lat_a, lat_b, to_a, to_b):
    out = jax.ShapeDtypeStruct((BULK + 24, LANES), jnp.float32)
    return pl.pallas_call(
        corner_pack_kernel,
        in_specs=[VMEM] * 4,
        out_specs=[VMEM] * 2,
        out_shape=[out, out],
        compiler_params=SMALL,
        name="corner_pack",
    )(lat_a, lat_b, to_a, to_b)


def main_kernel(
    stored, scale, levels, mask, cot, spin, lat_a, lat_b, lon_a, lon_b,
    lam, partial,
    m, m0, u0, u1, u2, u3, v0, v1, v2, v3, w0, w1, w2, w3, ea, eb, fe, q, la, lb, le,
    north, south,
):
    odd = lax.rem(lax.axis_index("lon"), 2) == 1
    upper = lax.rem(lax.axis_index("lat"), 2) == 1
    us, vs, ws = (u0, u1, u2, u3), (v0, v1, v2, v3), (w0, w1, w2, w3)
    fields = (m, m0, ea, u0, v0, le, la, lb)
    every = TILES + 1
    end = BASE + COLS

    for f in range(8):
        for row in (slice(0, 16), slice(96, HEIGHT)):
            fields[f][:, row] = jnp.zeros((every, 16, LANES), jnp.float32)
        for row in (slice(16, 24), slice(88, 96)):
            fields[f][:, row] = jnp.zeros((every, 8, LANES), jnp.float32)
    for t in range(TILES):
        at = slice(t * LANES, (t + 1) * LANES)
        own = own_fields(
            stored[:, :, at], scale[:, at], levels[:, at], mask[:, at], cot[:, :, at]
        )
        for f in range(8):
            fields[f][t, BASE:end] = own[f]
            width, place = LON_WIDTHS[f], t * SIDE + LON_PLACES[f]
            from_a, from_b = lon_a[place : place + width], lon_b[place : place + width]
            fields[f][t, BASE - width : BASE] = jnp.where(odd, from_a, from_b)
            fields[f][t, end : end + width] = jnp.where(odd, from_b, from_a)
    for n, (ref, own) in enumerate(((lat_a, lat_b), (lat_b, lat_a))):
        dst = (north, south)[n]
        dst[BASE:end] = jnp.where(upper, own[...], ref[...])
        first, second = (slice(BULK + k * WIDE, BULK + (k + 1) * WIDE) for k in (n, 1 - n))
        from_a = jnp.where(upper, lon_a[second], lon_a[first])
        from_b = jnp.where(upper, lon_b[second], lon_b[first])
        dst[BASE - WIDE : BASE] = jnp.where(odd, from_a, from_b)
        dst[end : end + WIDE] = jnp.where(odd, from_b, from_a)
    lane = lanes_of((COLS + 2 * WIDE, LANES))
    packs = [ref[BASE - WIDE : end + WIDE] for ref in (north, south)]
    for f in range(8):
        width, place = LAT_WIDTHS[f], LAT_PLACES[f]
        up = pltpu.roll(packs[0], (LANES - place) % LANES, 1) if place else packs[0]
        down = pltpu.roll(packs[1], LANES - width - place, 1)
        edge = jnp.where(lane < width, up, jnp.where(lane >= LANES - width, down, 0.0))
        fields[f][TILES, BASE - WIDE : end + WIDE] = edge

    first = lanes_of((every, 8, LANES)) == 0
    final = lanes_of((every, 8, LANES)) == LANES - 1

    def lat_diff(x):
        ahead = pltpu.roll(x, LANES - 1, 2)
        behind = pltpu.roll(x, 1, 2)
        ahead = jnp.where(final, jnp.concatenate([ahead[1:], ahead[:1]], axis=0), ahead)
        behind = jnp.where(first, jnp.concatenate([behind[-1:], behind[:-1]], axis=0), behind)
        return ahead - behind

    def lon_diff(ref, r):
        return ref[:, pl.ds(r + 1, 8)] - ref[:, pl.ds(r - 1, 8)]

    def sweep(start, stop, body):
        for r in range(start, stop, 8):
            body(r, pl.ds(r, 8))

    turn = spin[...]

    def start_step(r, here):
        w = m0[:, here] + m[:, here] * ea[:, here]
        w0[:, here] = w
        fe[:, here] = w * u0[:, here]

    sweep(8, 104, start_step)

    for k in range(STEPS - 1):
        e, s = (ea, eb) if k % 2 == 0 else (eb, ea)
        u, v, w, u_next, v_next, w_next = us[k], vs[k], ws[k], us[k + 1], vs[k + 1], ws[k + 1]
        lo, hi = ((8, 104), (8, 104), (16, 96))[k]
        lo_s, hi_s = ((8, 104), (8, 104), (16, 96))[k]
        if k == 1:
            lo, hi = 16, 96

        def height_pass(r, here):
            diverge = lon_diff(fe, r) + lat_diff(w[:, here] * v[:, here])
            s[:, here] = e[:, here] - (HALF * m[:, here]) * diverge

        sweep(lo_s, hi_s, height_pass)

        def speed_pass(r, here):
            ocean, height = m[:, here], s[:, here]
            old_u, old_v = u[:, here], v[:, here]
            new_u = ocean * (KEEP * old_u + turn * old_v - (GRAVITY * HALF) * lon_diff(s, r))
            new_v = ocean * (KEEP * old_v - turn * old_u - (GRAVITY * HALF) * lat_diff(height))
            u_next[:, here] = new_u
            v_next[:, here] = new_v
            new_w = m0[:, here] + ocean * height
            w_next[:, here] = new_w
            if k < STEPS - 2:
                fe[:, here] = new_w * new_u

        sweep(lo, hi, speed_pass)

    sums = [jnp.zeros((TILES, 8, LANES), jnp.float32) for _ in range(3)]
    for k in reversed(range(STEPS)):
        u, v, w, sb = us[k], vs[k], ws[k], fe

        def height_back(r, here):
            back = le[:, here] + (GRAVITY * HALF) * (lon_diff(la, r) + lat_diff(lb[:, here]))
            sb[:, here] = back
            q[:, here] = (HALF * m[:, here]) * back

        sweep(16, 96, height_back)

        def speed_back(r, here):
            g = lon_diff(q, r)
            h = lat_diff(q[:, here])
            a, b, depth = la[:, here], lb[:, here], w[:, here]
            new_a = KEEP * a - turn * b + depth * g
            new_b = KEEP * b + turn * a + depth * h
            new_e = sb[:, here] + m[:, here] * (u[:, here] * g + v[:, here] * h)
            if k > 0:
                la[:, here] = new_a
                lb[:, here] = new_b
                le[:, here] = new_e
                return
            own = slice(r - BASE, r - BASE + 8)
            for n, new in enumerate((new_e, new_a, new_b)):
                for t in range(TILES):
                    at = slice(t * LANES, (t + 1) * LANES)
                    lam[n, own, at] = new[t]
            half = (r - BASE) // 16 * 16
            for n, new in enumerate((new_e, new_a, new_b)):
                parts = []
                for t in range(TILES):
                    at = slice(t * LANES, (t + 1) * LANES)
                    block = stored[n, half : half + 16, at].astype(jnp.float32)
                    parts.append(new[t] * block[r - BASE - half : r - BASE - half + 8])
                sums[n] = sums[n] + jnp.stack(parts)

        if k > 0:
            sweep(16, 96, speed_back)
        else:
            sweep(BASE, BASE + COLS, speed_back)
    for n in range(3):
        total = jnp.sum(sums[n], axis=1)
        for t in range(TILES):
            partial[n : n + 1, t * LANES : (t + 1) * LANES] = total[t : t + 1]


def main(*operands):
    big = pltpu.VMEM((TILES + 1, HEIGHT, LANES), jnp.float32)
    return pl.pallas_call(
        main_kernel,
        in_specs=[VMEM] * 10,
        out_specs=[VMEM] * 2,
        out_shape=[
            jax.ShapeDtypeStruct((3, COLS, ROWS), jnp.float32),
            jax.ShapeDtypeStruct((3, ROWS), jnp.float32),
        ],
        scratch_shapes=[big] * 21 + [pltpu.VMEM((HEIGHT, LANES), jnp.float32)] * 2,
        compiler_params=pltpu.CompilerParams(vmem_limit_bytes=12 * 2**20),
        name="main",
    )(*operands)


def spin_table():
    total = ROWS * lax.axis_size("lat")
    lane = jnp.arange((TILES + 1) * LANES, dtype=jnp.int32)
    row = jnp.where(lane < ROWS + LANES // 2, lane, lane - (TILES + 1) * LANES)
    row = (row + lax.axis_index("lat") * ROWS).astype(jnp.float32)
    spin = CORIOLIS * jnp.cos(math.pi * (row + 0.5 - total) / (2.0 * total))
    spin = jnp.broadcast_to((TIME_STEP * spin).reshape(TILES + 1, 1, LANES), (TILES + 1, 8, LANES))
    return spin


def sum_over_lon(value):
    size = lax.axis_size("lon")
    columns = [[z * 8 + r for z in range(size // 8)] for r in range(8)]
    many = jnp.broadcast_to(value[None], (size // 8,) + value.shape)
    many = lax.all_to_all(many, "lon", 0, 0, axis_index_groups=columns)
    value = jnp.sum(many, axis=0)
    for steps in ((1,), (2, 4, 6)):
        value = value + sum(
            lax.ppermute(value, "lon", [(s, s ^ step) for s in range(size)]) for step in steps
        )
    return value


def shards(stored, scale, levels, mask, cot):
    lons, lats = lax.axis_size("lon"), lax.axis_size("lat")
    own = (stored, scale, levels, mask, cot)
    to_a, to_b = lat_pack(*own)
    lat_a = lax.ppermute(to_a, "lat", [(s, s ^ 1) for s in range(lats)])
    pairs = []
    for l in range(lons):
        for t in range(1, lats - 1, 2):
            pairs += [(l * lats + t, l * lats + t + 1), (l * lats + t + 1, l * lats + t)]
        pairs.append((l * lats + lats - 1, (lons - 1 - l) * lats + lats - 1))
    lat_b = lax.ppermute(to_b, ("lon", "lat"), pairs)
    bulk, near = lon_pack(own, to_b)
    to_a, to_b = corner_pack(lat_a, lat_b, *bulk)
    lon_a = lax.ppermute(to_a, "lon", [(s, s ^ 1) for s in range(lons)])
    lon_b = lax.ppermute(
        to_b, "lon", [(s, (s + 1) % lons if s % 2 else (s - 1) % lons) for s in range(lons)]
    )
    lam, partial = main(*near, spin_table(), lat_a, lat_b, lon_a, lon_b)
    return lam * near[1][:, None, :], sum_over_lon(partial)


def solution(mesh):
    return jax.shard_map(
        shards,
        mesh=mesh,
        in_specs=(
            P(None, "lon", "lat"),
            P(None, "lat"),
            P("lon", "lat"),
            P("lon", "lat"),
            P(None, "lon", "lat"),
        ),
        out_specs=(P(None, "lon", "lat"), P(None, "lat")),
        check_vma=False,
    )
```
